32 devices in a mesh: branch: 2 (over core), dp: 16 (over z, y, x).
Axes of the slice: x: 2, y: 2, z: 4, core: 2. Of those that a mesh axis runs over, the one named last changes fastest.
Arguments:
- block_input: bfloat16 [16384, 1024], P('dp', 'branch'), may hold values from -13.4 to 13.4
- cotangent: bfloat16 [16384, 1024], P('dp', 'branch'), may hold values from -6 to 6
- seq_lengths: int32 [16, 16], P('dp'), may hold values from 0 to 512, as said below
- layer_norm_gain: bfloat16 [1024], P('branch'), may hold values from 0.5 to 1.5
- layer_norm_bias: bfloat16 [1024], P('branch'), may hold values from -3 to 3
- qkv_weight: bfloat16 [1024, 3072], P('branch'), may hold values from -0.1875 to 0.1875
- out_weight: bfloat16 [1024, 1024], P('branch'), may hold values from -1.5 to 1.5
- in_weight: bfloat16 [1024, 4096], P('branch'), may hold values from -0.1875 to 0.1875
- in_bias: bfloat16 [4096], P('branch'), may hold values from -3 to 3
- back_weight: bfloat16 [4096, 1024], P('branch'), may hold values from -0.09375 to 0.09375
- back_bias: bfloat16 [1024], P('branch'), may hold values from -3 to 3
Outputs:
- block_output: bfloat16 [16384, 1024], P('dp', 'branch')
- input_grad: bfloat16 [16384, 1024], P('dp', 'branch')
- norm_gain_grad: float32 [1024], P('branch')
- norm_bias_grad: float32 [1024], P('branch')
- qkv_weight_grad: float32 [1024, 3072], P('branch')
- out_weight_grad: float32 [1024, 1024], P('branch')
- in_weight_grad: float32 [1024, 4096], P('branch')
- in_bias_grad: float32 [4096], P('branch')
- back_weight_grad: float32 [4096, 1024], P('branch')
- back_bias_grad: float32 [1024], P('branch')
The draws below stay inside these ranges and needn't reach their ends.
Inputs may be any that keep to these rules, and one draw needn't show every extreme that they name: `seq_lengths`: row s lists the lengths of the sequences packed in order from the first row of batch shard s, then zeros; every shard holds at least one sequence and rows after its last sequence are padding; some shard holds a sequence of exactly 512.
All inputs are finite; a program needn't handle non-finite values.
Results may differ from the reference program's by a relative error of at most 0.018.
Values may be sent and summed in bfloat16 or wider, within the bound.
A program may use at most 256 MiB of HBM per device.

```python
import math
import jax
import jax.numpy as jnp
from jax import lax

D = 1024
HEADS = 16
HEAD_DIM = 64
ROT = 32
FF = 4096
TOK_DEV = 1024
SLOTS = 16
SEQ_MAX = 512
SHARDS = 16
TOKENS = 16384


def draw_block_input(key, part):
    key = jax.random.fold_in(key, 5)
    subkeys = jax.random.split(key, 3)
    row_scale = jnp.exp(jax.random.uniform(subkeys[0], (TOKENS, 1), jnp.float32, 0.0, math.log(10.0)))
    column_scale = jnp.exp(jax.random.uniform(subkeys[1], (1, D), jnp.float32, 0.0, math.log(10.0)))
    entries = jnp.clip(jax.random.normal(subkeys[2], (TOKENS, D), jnp.float32), -4.0, 4.0)
    return (entries * row_scale * column_scale / 30.0).astype(jnp.bfloat16)


def draw_in_weight(key, part):
    key = jax.random.fold_in(key, 13)
    subkeys = jax.random.split(key, 2)
    entries = jnp.clip(jax.random.normal(subkeys[0], (D, FF), jnp.float32), -4.0, 4.0)
    common = jnp.clip(jax.random.normal(subkeys[1], (1, FF), jnp.float32), -4.0, 4.0)
    return ((entries + 0.5 * common) * D ** (-0.5)).astype(jnp.bfloat16)


def draw_seq_lengths(key, part):
    key = jax.random.fold_in(key, 9)
    subkeys = jax.random.split(key, 7)
    counts = jax.random.randint(subkeys[0], (SHARDS,), max(2, SLOTS // 2), SLOTS + 1)
    long_slot = jax.random.randint(subkeys[1], (SHARDS,), 0, counts)
    offset = jax.random.randint(subkeys[5], (SHARDS,), 1, counts)
    second_slot = (long_slot + offset) % counts
    spare = TOK_DEV - SEQ_MAX
    second_most = spare // 2
    short_most = (spare - second_most) // SLOTS
    shorter = jax.random.randint(subkeys[2], (SHARDS, SLOTS), 1, short_most + 1)
    second = jax.random.randint(subkeys[6], (SHARDS,), SEQ_MAX // 4, second_most + 1)
    longest = jax.random.randint(subkeys[3], (SHARDS,), 3 * SEQ_MAX // 4, SEQ_MAX + 1)
    chosen = jax.random.randint(subkeys[4], (), 0, SHARDS)
    longest = jnp.where(jnp.arange(SHARDS) == chosen, SEQ_MAX, longest)
    slot_index = jnp.arange(SLOTS)[None, :]
    lengths = jnp.where(slot_index < counts[:, None], shorter, 0)
    lengths = jnp.where(slot_index == second_slot[:, None], second[:, None], lengths)
    lengths = jnp.where(slot_index == long_slot[:, None], longest[:, None], lengths)
    return lengths.astype(jnp.int32)


def level_of(stream_key, shape, cuts, low, largest):
    def one(axis_at, shards_of):
        steps = jax.random.uniform(jax.random.fold_in(jax.random.fold_in(stream_key, 6), axis_at), (shards_of,), jnp.float32, low / len(cuts), largest / len(cuts))
        return jnp.repeat(jnp.exp(steps), shape[axis_at] // shards_of).reshape((-1,) + (1,) * (len(shape) - axis_at - 1))

    factor_of = one(*cuts[0])
    for cut in cuts[1:]:
        factor_of = factor_of * one(*cut)
    return factor_of


def scatter_about(own_key, shape, spread, most, shards=(), held_as=jnp.bfloat16):
    gain = level_of(own_key, shape, shards, -0.22, 0.18) if shards else 1.0
    values = jax.random.normal(own_key, shape, jnp.float32) * spread * gain
    return jnp.minimum(jnp.maximum(values, -most), most).astype(held_as)


def setup_inputs(seed: int = 0) -> dict:
    streams_of = jax.random.split(jax.random.key(seed), 12)
    return {
        "block_input": draw_block_input(jax.random.fold_in(streams_of[11], 71), 0),
        "cotangent": scatter_about(streams_of[1], (TOKENS, D), 1.0, 6.0, ((0, 16), (1, 2))),
        "seq_lengths": draw_seq_lengths(jax.random.fold_in(streams_of[11], 71), 0),
        "layer_norm_gain": jnp.clip(1.0 + 0.1 * jax.random.normal(streams_of[3], (D,), jnp.float32), 0.5, 1.5).astype(jnp.bfloat16),
        "layer_norm_bias": scatter_about(streams_of[4], (D,), 0.5, 3.0, ((0, 2),)),
        "qkv_weight": scatter_about(streams_of[5], (D, 3 * D), D ** -0.5, 0.1875, ((0, 2),)),
        "out_weight": scatter_about(streams_of[6], (D, D), (D // 64) ** -0.5, 1.5, ((0, 2),)),
        "in_weight": draw_in_weight(jax.random.fold_in(streams_of[11], 71), 0),
        "in_bias": scatter_about(streams_of[8], (FF,), 0.5, 3.0, ((0, 2),)),
        "back_weight": scatter_about(streams_of[9], (FF, D), FF ** -0.5, 0.09375, ((0, 2),)),
        "back_bias": scatter_about(streams_of[10], (D,), 0.5, 3.0, ((0, 2),)),
    }


@jax.custom_vjp
def reduced_precision(v):
    return lax.optimization_barrier(v.astype(jnp.bfloat16)).astype(jnp.float32)

@jax.custom_vjp
def low_back(v):
    return v

def low_keep(v):
    return (reduced_precision(v), None)

def low_pass(kept, grad):
    return (grad,)

def back_keep(v):
    return (v, None)

def back_low(kept, grad):
    return (reduced_precision(grad),)
reduced_precision.defvjp(low_keep, low_pass)
low_back.defvjp(back_keep, back_low)
NORM_EPSILON = 1e-05
MASKED = -1e+30
PRECISE = lax.Precision.HIGHEST

def both_ways(values):
    return reduced_precision(low_back(values))

def layout(lengths):
    ends = jnp.cumsum(lengths, dtype=jnp.int32)
    place = jnp.arange(TOK_DEV, dtype=jnp.int32)
    passed = (place[:, None] >= ends[None, :]).astype(jnp.int32)
    segment = lax.optimization_barrier(jnp.sum(passed, axis=1, dtype=jnp.int32))
    starts = lax.optimization_barrier(jnp.sum(passed * lengths[None, :], axis=1, dtype=jnp.int32))
    position = (place - starts).astype(jnp.float32)
    live_rows = (place < ends[-1]).astype(jnp.float32)
    return (segment, position, live_rows)

def tables(position):
    column = jnp.arange(D, dtype=jnp.int32) % HEAD_DIM
    pair_index = (column // 2).astype(jnp.float32)
    frequency = jnp.exp(pair_index * (-2.0 * math.log(10000.0) / ROT))
    angles = position[:, None] * frequency[None, :]
    rotated = (column < ROT)[None, :]
    sign_flip = jnp.where(column % 2 == 0, -1.0, 1.0)[None, :]
    cosine_table = jnp.where(rotated, jnp.cos(angles), 1.0)
    sine_table = jnp.where(rotated, jnp.sin(angles) * sign_flip, 0.0)
    return (cosine_table, sine_table)

def swap_pairs(values):
    even_column = (jnp.arange(values.shape[1]) % 2 == 0)[None, :]
    return jnp.where(even_column, jnp.roll(values, -1, axis=1), jnp.roll(values, 1, axis=1))

def rotate(values, cosine_table, sine_table):
    return values * cosine_table + swap_pairs(values) * sine_table

def shard_forward(inputs, segment, position, live_rows, params):
    layer_norm_gain, layer_norm_bias, qkv_weight, out_weight, in_weight, in_bias, back_weight, back_bias = params
    row_mean = lax.optimization_barrier(jnp.mean(inputs, axis=1, keepdims=True))
    centered_input = inputs - row_mean
    feature_variance = lax.optimization_barrier(jnp.mean(centered_input * centered_input, axis=1, keepdims=True))
    standardized_input = centered_input * lax.rsqrt(feature_variance + NORM_EPSILON)
    normalized_input = reduced_precision(standardized_input * layer_norm_gain + layer_norm_bias)
    projected = jnp.dot(normalized_input, qkv_weight, precision=PRECISE)
    cosine_table, sine_table = tables(position)
    queries = reduced_precision(rotate(low_back(projected[:, :D]), cosine_table, sine_table))
    key_rows = reduced_precision(rotate(low_back(projected[:, D:2 * D]), cosine_table, sine_table))
    values = both_ways(projected[:, 2 * D:])
    query_heads = queries.reshape(TOK_DEV, HEADS, HEAD_DIM)
    key_heads = key_rows.reshape(TOK_DEV, HEADS, HEAD_DIM)
    value_heads = values.reshape(TOK_DEV, HEADS, HEAD_DIM)
    place = jnp.arange(TOK_DEV, dtype=jnp.int32)
    allowed = (segment[:, None] == segment[None, :]) & (place[None, :] <= place[:, None]) & (live_rows[None, :] > 0.5)
    allowed = allowed | (place[None, :] == place[:, None])
    scores = low_back(jnp.einsum('qhd,khd->hqk', query_heads, key_heads, precision=PRECISE) * HEAD_DIM ** (-0.5))
    scores = jnp.where(allowed[None], scores, MASKED)
    row_top = lax.optimization_barrier(jnp.max(scores, axis=2, keepdims=True))
    exponent = jnp.exp(scores - row_top)
    attention = exponent / lax.optimization_barrier(jnp.sum(exponent, axis=2, keepdims=True))
    context = jnp.einsum('hqk,khd->qhd', reduced_precision(attention), value_heads, precision=PRECISE)
    context = both_ways(context.reshape(TOK_DEV, D))
    attended = reduced_precision(jnp.dot(context, out_weight, precision=PRECISE))
    hidden = low_back(jnp.dot(normalized_input, in_weight, precision=PRECISE) + in_bias)
    active = reduced_precision(jax.nn.gelu(hidden, approximate=True))
    mixed = reduced_precision(jnp.dot(active, back_weight, precision=PRECISE) + back_bias)
    return inputs + (attended + mixed)

def reference(block_input, cotangent, seq_lengths, layer_norm_gain, layer_norm_bias, qkv_weight, out_weight, in_weight, in_bias, back_weight, back_bias):
    segment, position, live_rows = jax.vmap(layout)(seq_lengths)
    inputs = block_input.astype(jnp.float32).reshape(SHARDS, TOK_DEV, D)
    params = tuple((weight.astype(jnp.float32) for weight in (layer_norm_gain, layer_norm_bias, qkv_weight, out_weight, in_weight, in_bias, back_weight, back_bias)))

    def forward(inputs, params):

        def one_shard(shard_item):
            return shard_forward(shard_item[0], shard_item[1], shard_item[2], shard_item[3], params)
        return lax.map(jax.checkpoint(one_shard), (inputs, segment, position, live_rows))
    outputs, pull_back = jax.vjp(forward, inputs, params)
    masked_cot = cotangent.astype(jnp.float32).reshape(SHARDS, TOK_DEV, D) * live_rows[:, :, None]
    input_grad, grads = pull_back(masked_cot)
    gain_grad, shift_grad, qkv_grad, out_grad, in_grad, in_bias_grad, back_grad, back_bias_grad = grads
    return (outputs.reshape(TOKENS, D).astype(jnp.bfloat16), input_grad.reshape(TOKENS, D).astype(jnp.bfloat16), gain_grad, shift_grad, qkv_grad, out_grad, in_grad, in_bias_grad, back_grad, back_bias_grad)
```

```python
import functools
import math

import jax
import jax.numpy as jnp
from jax import lax
from jax.experimental import pallas as pl
from jax.experimental.pallas import tpu as pltpu
from jax.sharding import PartitionSpec as P

HEAD_DIM = 64
ROT = 32
NORM_EPSILON = 1e-05
MASKED = -1e30
PAD_CODE = 1 << 16
TILE = 256
PAIR = 128
MESH = pl.DeviceIdType.MESH
F32 = jnp.float32
BF16 = jnp.bfloat16
ROOT = math.sqrt(2.0 / math.pi)
CUBIC = 0.044715


def ds(start, size):
    if not isinstance(start, int):
        for unit in (1024, 512, 256, 128, 64, 32, 16, 8):
            if size % unit == 0:
                start = pl.multiple_of(start, unit)
                break
    return pl.ds(start, size)


def dot(a, b):
    return lax.dot_general(a, b, (((1,), (0,)), ((), ())), preferred_element_type=F32)


def dot_nt(a, b):
    return lax.dot_general(a, b, (((1,), (1,)), ((), ())), preferred_element_type=F32)


def dot_tn(a, b):
    return lax.dot_general(a, b, (((0,), (0,)), ((), ())), preferred_element_type=F32)


def loop(count, body):
    def step(i, carry):
        body(i)
        return carry

    lax.fori_loop(0, count, step, 0)


def inside(value, count):
    return (value >= 0) & (value < count)


def dp_lines(mesh):
    count = mesh.shape["dp"]
    places = [getattr(d, "coords", None) for d in mesh.devices[0]]
    lines = []
    if all(p is not None for p in places):
        for axis in range(3):
            length = len({p[axis] for p in places})
            if length > 1:
                first = next(i for i in range(count) if places[i][axis] != places[0][axis])
                lines.append((first, length))
        lines.sort()
        stride = 1
        for s, n in lines:
            if s != stride:
                lines = []
                break
            stride *= n
        if lines and stride == count:
            return lines
    lines, stride = [], 1
    while stride < count:
        lines.append((stride, 2))
        stride *= 2
    return lines


class Line:
    def __init__(self, dp, stride, length):
        self.dp, self.stride, self.length = dp, stride, length
        self.place = lax.rem(lax.div(dp, stride), length)

    def at(self, step):
        return {"dp": self.dp + step * self.stride}


def line_sems(length):
    return 1 if length == 2 else 2 * (length - 1)


def land_rows(rows, lengths):
    need = 0
    for length in lengths:
        rows //= length
        need += rows * line_sems(length)
    return need


class Wire:
    def __init__(self, send, recv):
        self.send, self.recv, self.used, self.sent = send, recv, 0, []

    def take(self):
        self.used += 1
        return self.used - 1

    def copy(self, src, dst, sem, to):
        return pltpu.make_async_remote_copy(
            src_ref=src,
            dst_ref=dst,
            send_sem=self.send.at[sem],
            recv_sem=self.recv.at[sem],
            device_id=to,
            device_id_type=MESH,
        )

    def finish(self):
        for can, build in self.sent:
            if can is None:
                build().wait_send()
            else:
                pl.when(can)(lambda build=build: build().wait_send())
        self.sent = []


class Rows:
    def __init__(self, ref, column, width):
        self.ref, self.column, self.width = ref, column, width

    def at(self, row, rows):
        return self.ref.at[ds(row, rows), pl.ds(self.column, self.width)]

    def load(self, row, rows):
        return self.ref[ds(row, rows), pl.ds(self.column, self.width)]

    def store(self, row, rows, value):
        self.ref[ds(row, rows), pl.ds(self.column, self.width)] = value


def add_rows(block, base, land, off, rows):
    step = next(s for s in (64, 48, 32, 16) if rows % s == 0)

    even = math.gcd(off, step)

    def body(i):
        mine = block.load(base + i * step, step).astype(F32)
        at = pl.multiple_of(off + i * step, even) if even > 1 and not isinstance(i, int) else off
        other = land.ref[pl.ds(at, step), pl.ds(land.column, land.width)].astype(F32)
        block.store(base + i * step, step, (mine + other).astype(BF16))

    if rows == step:
        body(0)
    else:
        loop(rows // step, body)


def sum_line(wire, line, block, base, rows, land, off):
    length, p = line.length, line.place
    blk = rows // length
    if length == 2:
        sem = wire.take()
        other = 1 - p

        def build():
            return wire.copy(
                block.at(base + other * blk, blk), land.at(off, blk), sem, line.at(1 - 2 * p)
            )

        build().start()
        wire.sent.append((None, build))
        yield
        build().wait_recv()
        add_rows(block, base + p * blk, land, off, blk)
        return
    for s in range(1, length):
        r = length - s
        todo = []
        for d in (-1, 1):
            sem = wire.take()
            low = off + (2 * (s - 1) + (d > 0)) * blk

            def build(owner, d=d, sem=sem, low=low):
                return wire.copy(
                    block.at(base + owner * blk, blk), land.at(low, blk), sem, line.at(d)
                )

            can = inside(p + d * r, length)
            goes = functools.partial(build, p + d * r)
            pl.when(can)(lambda goes=goes: goes().start())
            wire.sent.append((can, goes))
            todo.append((d, build, low))
        yield
        for d, build, low in todo:
            owner = p - d + d * r

            def arrive(build=build, owner=owner, low=low):
                build(owner).wait_recv()
                add_rows(block, base + owner * blk, land, low, blk)

            pl.when(inside(p - d, length) & inside(owner, length))(arrive)


def spread_line(wire, line, out, base, blk, first=None):
    length, p = line.length, line.place
    if length == 2:
        sem = wire.take()

        def build(owner, source=None):
            there = out.at(base + owner * blk, blk)
            return wire.copy(there if source is None else source, there, sem, line.at(1 - 2 * p))

        goes = functools.partial(build, p, first)
        goes().start()
        wire.sent.append((None, goes))
        yield
        build(1 - p).wait_recv()
        return
    for r in range(1, length):
        todo = []
        for d in (-1, 1):
            sem = wire.take()

            def build(owner, source=None, d=d, sem=sem):
                there = out.at(base + owner * blk, blk)
                return wire.copy(there if source is None else source, there, sem, line.at(d))

            owner = p - d * (r - 1)
            can = inside(owner, length) & inside(p + d, length)
            goes = functools.partial(build, owner, first if r == 1 else None)
            pl.when(can)(lambda goes=goes: goes().start())
            wire.sent.append((can, goes))
            todo.append((d, build))
        yield
        for d, build in todo:
            owner = p - d * r
            pl.when(inside(owner, length))(
                lambda build=build, owner=owner: build(owner).wait_recv()
            )


def unit_flow(wire, order, block, row, rows, land, off, out, local_sem):
    base, size, spots = row, rows, []
    for line in order:
        yield from sum_line(wire, line, block, base, size, land, off)
        size //= line.length
        off += size * line_sems(line.length)
        spots.append((base, size))
        base = base + line.place * size
    own = pltpu.make_async_copy(block.at(base, size), out.at(base, size), local_sem)
    own.start()
    first = block.at(base, size)
    for line, (start, blk) in list(zip(order, spots))[::-1]:
        yield from spread_line(wire, line, out, start, blk, first)
        if first is not None:
            own.wait()
        first = None


def vector_flow(wire, lines, vec, slots):
    for line, slot in zip(lines, slots):
        rows = vec.shape[0]
        slot[ds(line.place * rows, rows), :] = vec[...]
        yield from spread_line(wire, line, Rows(slot, 0, slot.shape[1]), 0, rows)
        total = slot[0:rows, :]
        for k in range(1, line.length):
            total = total + slot[k * rows : (k + 1) * rows, :]
        vec[...] = total


BACK, IN, OUT, QKV = 0, 1, 2, 3


def make_units():
    units = []
    for part in range(4):
        units += [(BACK, 512 * part, 0), (BACK, 512 * part + 256, 0)]
        if part % 2:
            for c in (part // 2, 2 + part // 2):
                units += [(IN, 0, 1024 * c), (IN, 256, 1024 * c)]
    units += [(OUT, 0, 0), (OUT, 256, 0)]
    for c in range(3):
        units += [(QKV, 0, 1024 * c), (QKV, 256, 1024 * c)]
    return units


UNITS = make_units()
FEED_UNITS = 16
ORDERS = "XYZXYZXYZXYZXYZX" + "XYXYXYXY"


def line_order(letter, lines):
    k = len(lines)
    first = min("XYZ".index(letter), k - 1)
    return [first] + [i for i in range(k) if i != first]


def rotate_pairs(values, even):
    return jnp.where(
        even, pltpu.roll(values, PAIR - 1, axis=1), pltpu.roll(values, 1, axis=1)
    )


def kernel(
    lines_at,
    summed,
    plan,
    x_hbm,
    cot_hbm,
    qkv_hbm,
    out_hbm,
    in_hbm,
    back_hbm,
    small_ref,
    in_bias_ref,
    code_col,
    code_row,
    cosine,
    sine,
    block_out,
    input_grad,
    vec,
    back_res,
    in_res,
    out_res,
    qkv_res,
    qkv_other,
    x_far,
    x,
    cot,
    normed,
    turned,
    wa,
    wb,
    act,
    gh,
    mix,
    gn,
    stage,
    act_t,
    acc,
    small,
    g_back,
    g_in,
    g_out,
    g_qkv,
    land,
    slots_x,
    slots_y,
    slots_z,
    core_send,
    core_recv,
    local,
    send,
    recv,
    own_sems,
    core_free,
    land_free,
):
    rows = x.shape[0]
    half = x.shape[1] // 2
    side = lax.axis_index("branch")
    dp = lax.axis_index("dp")
    mate = {"branch": 1 - side}
    lines = [Line(dp, s, n) for s, n in lines_at]
    core = Wire(core_send, core_recv)
    wire = Wire(send, recv)
    mine, theirs = side * half, (1 - side) * half

    barrier = pltpu.get_barrier_semaphore()
    pl.semaphore_signal(barrier, inc=1, device_id=mate, device_id_type=MESH)
    greeted = jnp.int32(1)

    def each_neighbour(visit):
        count = jnp.int32(0)
        for line in lines:
            for d in (-1, 1):
                there = inside(line.place + d, line.length)
                pl.when(there)(lambda line=line, d=d: visit(line.at(d)))
                count = count + there.astype(jnp.int32)
        return count

    if summed:
        greeted = greeted + each_neighbour(
            lambda to: pl.semaphore_signal(barrier, inc=1, device_id=to, device_id_type=MESH)
        )

    loads = []

    def load(src, dst):
        c = pltpu.make_async_copy(src, dst, local.at[len(loads)])
        c.start()
        loads.append(c)
        return c

    x_in = load(x_hbm, x.at[:, ds(mine, half)])
    in_in = load(in_hbm.at[:, ds(side * 4 * half, 4 * half)], wa.at[ds(mine, half), :])
    cot_in = load(cot_hbm, cot.at[:, ds(mine, half)])
    back_in = load(back_hbm, wb)
    pl.semaphore_wait(barrier, greeted)

    def to_mate(src, dst):
        sem = core.take()

        def build():
            return core.copy(src, dst, sem, mate)

        build().start()
        core.sent.append((None, build))
        return build

    def from_mate(build, dst):
        return lambda: build().wait_recv()

    x_other = to_mate(x_hbm, x.at[:, ds(mine, half)])
    small_other = to_mate(small_ref, small.at[1])
    in_other = [
        to_mate(
            in_hbm.at[:, ds((1 - side) * 4 * half + k * 512, 512)],
            wa.at[ds(mine, half), pl.ds(k * 512, 512)],
        )
        for k in range(4)
    ]
    cot_other = to_mate(cot_hbm, cot.at[:, ds(mine, half)])
    qkv_far = [
        to_mate(
            qkv_hbm.at[:, ds(k * 2 * half + theirs, half)],
            qkv_other.at[:, pl.ds(k * half, half)],
        )
        for k in range(3)
    ]

    x_again = to_mate(x_hbm, x_far)

    x_in.wait()
    x_other().wait_recv()
    small_other().wait_recv()
    gain_mine = small_ref[0:1, :].astype(F32)
    shift_mine = small_ref[1:2, :].astype(F32)
    gain_other = small[1, 0:1, :].astype(F32)
    shift_other = small[1, 1:2, :].astype(F32)
    first = side == 0

    def both(own, other):
        return jnp.concatenate(
            [jnp.where(first, own, other), jnp.where(first, other, own)], axis=1
        )

    gain = both(gain_mine, gain_other)
    shift = both(shift_mine, shift_other)

    def standard(values):
        mean = jnp.mean(values, axis=1, keepdims=True)
        centred = values - mean
        variance = jnp.mean(centred * centred, axis=1, keepdims=True)
        scale = lax.rsqrt(variance + NORM_EPSILON)
        return mean, scale, centred * scale

    def norm_tile(i):
        at = ds(i * 128, 128)
        _, _, xhat = standard(x[at, :].astype(F32))
        value = xhat * gain + shift
        normed[at, :] = value.astype(BF16)
        turned[:, at] = value.T.astype(BF16)

    loop(rows // 128, norm_tile)

    def give_land(which):
        if summed:
            each_neighbour(
                lambda to: pl.semaphore_signal(
                    land_free.at[which], inc=1, device_id=to, device_id_type=MESH
                )
            )

    def take_land(which):
        if summed:
            pl.semaphore_wait(land_free.at[which], each_neighbour(lambda to: None))

    give_land(0)
    cot_in.wait()
    cot_other().wait_recv()

    def live_tile(i):
        at = ds(i * 128, 128)
        live = code_col[at, :] < PAD_CODE
        cot[at, :] = jnp.where(live, cot[at, :].astype(F32), 0.0).astype(BF16)

    loop(rows // 128, live_tile)
    in_in.wait()
    back_in.wait()

    stage_sends = {}

    def send_stage(name, slot, view, dst):
        sem = core.take()

        def build():
            return core.copy(view, dst, sem, mate)

        build().start()
        stage_sends[slot] = build
        return build

    def hidden_block(j):
        at = pl.ds(j * TILE, TILE)

        def row_tile(m, total):
            r = ds(m * TILE, TILE)
            hidden = dot(normed[r, :], wa[:, at]) + in_bias_ref[j : j + 1, :]
            square = hidden * hidden
            t = jnp.tanh(ROOT * hidden * (1.0 + CUBIC * square))
            up = 0.5 * (1.0 + t)
            active = hidden * up
            slope = up + 0.5 * hidden * (1.0 - t * t) * (ROOT * (1.0 + 3.0 * CUBIC * square))
            act[r, at] = active.astype(BF16)
            act_t[:, r] = active.T.astype(BF16)
            grad = dot_nt(cot[r, :], wb[at, :]) * slope
            low = grad.astype(BF16)
            gh[r, at] = low
            return total + jnp.sum(low.astype(F32), axis=0, keepdims=True)

        total = lax.fori_loop(0, rows // TILE, row_tile, jnp.zeros((1, TILE), F32))
        vec[j : j + 1, :] = total

        def back_tile(n):
            c = ds(n * TILE, TILE)
            g_back[at, c] = dot(act_t[...], cot[:, c]).astype(BF16)

        loop(2 * half // TILE, back_tile)
        slot = j % 2
        if slot in stage_sends:
            stage_sends[slot]().wait_send()

        def in_tile(n):
            g_in[ds(n * TILE, TILE), ds(side * 4 * half + j * TILE, TILE)] = dot(
                turned[ds(mine + n * TILE, TILE), :], gh[:, at]
            ).astype(BF16)
            stage[slot, ds(n * TILE, TILE), pl.ds(0, TILE)] = dot(
                turned[ds(theirs + n * TILE, TILE), :], gh[:, at]
            ).astype(BF16)

        loop(half // TILE, in_tile)
        return send_stage(
            "in",
            slot,
            stage.at[slot, :, pl.ds(0, TILE)],
            g_in.at[:, ds(side * 4 * half + j * TILE, TILE)],
        )

    in_swaps = []

    def feed_part(part):
        in_other[part]().wait_recv()
        for j in (2 * part, 2 * part + 1):
            in_swaps.append(hidden_block(j))

    def swap_wait(builds):
        for build in builds:
            build().wait_recv()

    def feed_out(m):
        r = ds(m * TILE, TILE)
        for n in range(2):
            c = pl.ds(n * 512, 512)
            mix[r, c] = dot(act[r, :], wb[:, c]).astype(BF16)
            gn[r, c] = dot_nt(gh[r, :], wa[c, :]).astype(BF16)

    late = []

    def feed_close():
        loop(rows // TILE, feed_out)
        for build in qkv_far:
            build().wait_recv()
        base = len(loads)
        for k in range(3):
            late.append(
                load(
                    qkv_hbm.at[:, ds(k * 2 * half + mine, half)],
                    wa.at[ds(mine, half), pl.ds(k * half, half)],
                )
            )
        late.append(load(qkv_other, wa.at[ds(theirs, half), pl.ds(0, 3 * half)]))
        late.append(load(out_hbm, wb.at[pl.ds(0, half), :]))
        pl.semaphore_signal(core_free, inc=1, device_id=mate, device_id_type=MESH)

    even = lax.rem(lax.broadcasted_iota(jnp.int32, (1, PAIR), 1), 2) == 0

    def project(m):
        r = ds(m * TILE, TILE)
        cos_t, sin_t = cosine[r, :], sine[r, :]
        for k in range(3):
            made = dot(normed[r, :], wa[:, pl.ds(k * half, half)])
            if k == 2:
                act[r, pl.ds(2 * half, half)] = made.astype(BF16)
                continue
            for c in range(half // PAIR):
                piece = made[:, c * PAIR : (c + 1) * PAIR]
                piece = piece * cos_t + rotate_pairs(piece, even) * sin_t
                if k == 0:
                    piece = piece * HEAD_DIM**-0.5
                act[r, pl.ds(k * half + c * PAIR, PAIR)] = piece.astype(BF16)
        act[r, pl.ds(3 * half, half)] = dot_nt(cot[r, :], wb[pl.ds(0, half), :]).astype(BF16)

    def project_all():
        for c in late:
            c.wait()
        loop(rows // TILE, project)
        give_land(1)

    lane = lax.broadcasted_iota(jnp.int32, (1, PAIR), 1)

    def unrotate(grad, r):
        return grad * cosine[r, :] + rotate_pairs(grad * sine[r, :], even)

    def attend_block(pair, i):
        low = max(0, i - 2) * TILE
        count = (i + 1) * TILE - low
        qr, kr = pl.ds(i * TILE, TILE), pl.ds(low, count)
        qc = ds(pair * PAIR, PAIR)
        kc = ds(half + pair * PAIR, PAIR)
        vc = ds(2 * half + pair * PAIR, PAIR)
        gc = ds(3 * half + pair * PAIR, PAIR)
        q, k, v, g = act[qr, qc], act[kr, kc], act[kr, vc], act[qr, gc]
        same = code_col[qr, :] == code_row[:, kr]
        place_q = i * TILE + lax.broadcasted_iota(jnp.int32, (TILE, count), 0)
        place_k = low + lax.broadcasted_iota(jnp.int32, (TILE, count), 1)
        allowed = same & (place_k <= place_q)
        context = jnp.zeros((TILE, PAIR), F32)
        grad_q = jnp.zeros((TILE, PAIR), F32)
        grad_k = jnp.zeros((count, PAIR), F32)
        grad_v = jnp.zeros((count, PAIR), F32)
        zero = jnp.zeros((), BF16)
        for head in range(2):
            here = (lane >= head * HEAD_DIM) & (lane < (head + 1) * HEAD_DIM)
            kh, vh = jnp.where(here, k, zero), jnp.where(here, v, zero)
            qh, gr = jnp.where(here, q, zero), jnp.where(here, g, zero)
            scores = jnp.where(allowed, dot_nt(q, kh), MASKED)
            top = jnp.max(scores, axis=1, keepdims=True)
            weight = jnp.exp(scores - top)
            weight = weight * (1.0 / jnp.sum(weight, axis=1, keepdims=True))
            weight_low = weight.astype(BF16)
            context = context + dot(weight_low, vh)
            grad_weight = dot_nt(g, vh)
            inner = jnp.sum(weight * grad_weight, axis=1, keepdims=True)
            grad_scores = (weight * (grad_weight - inner)).astype(BF16)
            grad_v = grad_v + dot_tn(weight_low, gr)
            grad_q = grad_q + dot(grad_scores, kh)
            grad_k = grad_k + dot_tn(grad_scores, qh)
        act[qr, gc] = context.astype(BF16)
        act[qr, qc] = unrotate(grad_q * HEAD_DIM**-0.5, qr).astype(BF16)
        fresh = count if i < 1 else TILE
        old = count - TILE
        if old:
            acc[0, pl.ds(low, old), :] += grad_k[:old]
            acc[1, pl.ds(low, old), :] += grad_v[:old]
        acc[0, pl.ds(low + old, TILE), :] = grad_k[old:]
        acc[1, pl.ds(low + old, TILE), :] = grad_v[old:]

    def attend_pair(pair):
        for i in range(rows // TILE):
            attend_block(pair, i)

        def close(m):
            r = ds(m * TILE, TILE)
            act[r, ds(half + pair * PAIR, PAIR)] = unrotate(acc[0, r, :], r).astype(BF16)
            act[r, ds(2 * half + pair * PAIR, PAIR)] = acc[1, r, :].astype(BF16)

        loop(rows // TILE, close)

    def out_grad():
        def tile(n):
            c = ds(n * TILE, TILE)
            g_out[:, c] = dot_tn(act[:, pl.ds(3 * half, half)], cot[:, c]).astype(BF16)

        loop(2 * half // TILE, tile)

    qkv_swaps = []

    def qkv_grad(k):
        slot = k % 2
        if slot in stage_sends:
            stage_sends[slot]().wait_send()

        def tile(n):
            r = ds(n * TILE, TILE)
            right = act[:, pl.ds(k * half, half)]
            g_qkv[r, ds(k * 2 * half + mine, half)] = dot(
                turned[ds(mine + n * TILE, TILE), :], right
            ).astype(BF16)
            stage[slot, r, :] = dot(turned[ds(theirs + n * TILE, TILE), :], right).astype(BF16)

        loop(half // TILE, tile)
        qkv_swaps.append(
            send_stage("qkv", slot, stage.at[slot], g_qkv.at[:, ds(k * 2 * half + mine, half)])
        )

    swaps = []

    def totals():
        x_again().wait_recv()
        late.append(load(x_hbm, turned.at[:, ds(mine, half)]))
        late.append(load(x_far, turned.at[:, ds(theirs, half)]))

        def tile(m):
            r = ds(m * TILE, TILE)
            for n in range(2):
                c = pl.ds(n * 512, 512)
                mix[r, c] = (
                    mix[r, c].astype(F32)
                    + dot(act[r, pl.ds(3 * half, half)], wb[pl.ds(0, half), c])
                ).astype(BF16)
                gn[r, c] = (
                    gn[r, c].astype(F32)
                    + dot_nt(act[r, pl.ds(0, 3 * half)], wa[c, pl.ds(0, 3 * half)])
                ).astype(BF16)

        loop(rows // TILE, tile)
        pl.semaphore_wait(core_free, 1)
        for src, dst in (
            (gn, gh.at[:, pl.ds(0, 2 * half)]),
            (mix.at[:, ds(theirs, half)], gh.at[:, pl.ds(2 * half, half)]),
        ):
            swaps.append(to_mate(src, dst))

    def last():
        for build in swaps:
            build().wait_recv()
        for c in late[-2:]:
            c.wait()
        back_bias = small_ref[2:3, :].astype(F32)
        own = ds(mine, half)

        def tile(m, carry):
            gain_sum, shift_sum, bias_sum = carry
            r = ds(m * 128, 128)
            mean, scale, xhat = standard(turned[r, :].astype(F32))
            x_own = turned[r, own].astype(F32)
            gh[r, pl.ds(3 * half, half)] = (
                x_own
                + (mix[r, own].astype(F32) + gh[r, pl.ds(2 * half, half)].astype(F32) + back_bias)
            ).astype(BF16)
            scaled = (gn[r, :].astype(F32) + gh[r, pl.ds(0, 2 * half)].astype(F32)) * gain
            mean_one = jnp.mean(scaled, axis=1, keepdims=True)
            mean_two = jnp.mean(scaled * xhat, axis=1, keepdims=True)
            grad_own = gn[r, own].astype(F32) + gh[r, own].astype(F32)
            xhat_own = (x_own - mean) * scale
            cot_own = cot[r, own].astype(F32)
            cot[r, own] = (
                cot_own + scale * (grad_own * gain_mine - mean_one - xhat_own * mean_two)
            ).astype(BF16)
            return (
                gain_sum + jnp.sum(grad_own * xhat_own, axis=0, keepdims=True),
                shift_sum + jnp.sum(grad_own, axis=0, keepdims=True),
                bias_sum + jnp.sum(cot_own, axis=0, keepdims=True),
            )

        zero = jnp.zeros((1, half), F32)
        gain_sum, shift_sum, bias_sum = lax.fori_loop(0, rows // 128, tile, (zero, zero, zero))
        for k, value in enumerate((bias_sum, gain_sum, shift_sum)):
            vec[8 + 2 * k : 9 + 2 * k, :] = value[:, :TILE]
            vec[9 + 2 * k : 10 + 2 * k, :] = value[:, TILE:]
        vec[14:16, :] = jnp.zeros((2, TILE), F32)
        late.append(load(gh.at[:, pl.ds(3 * half, half)], block_out))
        late.append(load(cot.at[:, ds(mine, half)], input_grad))

    results = {BACK: back_res, IN: in_res, OUT: out_res, QKV: qkv_res}
    grads = {BACK: g_back, IN: g_in, OUT: g_out, QKV: g_qkv}
    flows = {}
    if summed:
        off = 0
        lengths = [n for _, n in lines_at]
        for u, (kind, row, column) in enumerate(UNITS):
            order = line_order(plan["orders"][u], lines_at)
            need = land_rows(TILE, [lengths[i] for i in order])
            where = plan["land"][u]
            zone = Rows({"land": land, "wb": wb, "normed": normed, "x": x}[where[0]], 0, 1024)
            flows[u] = unit_flow(
                wire,
                [lines[i] for i in order],
                Rows(grads[kind], column, 1024),
                row,
                TILE,
                zone,
                where[1],
                Rows(results[kind], column, 1024),
                own_sems.at[u],
            )
        flows["vec"] = vector_flow(wire, lines, vec, (slots_x, slots_y, slots_z)[: len(lines)])

    steps = {
        "feed0": lambda: feed_part(0),
        "feed1": lambda: feed_part(1),
        "swap01": lambda: swap_wait(in_swaps[0:4]),
        "feed2": lambda: feed_part(2),
        "feed3": lambda: feed_part(3),
        "swap23": lambda: swap_wait(in_swaps[4:8]),
        "close": feed_close,
        "project": project_all,
        "pair0": lambda: attend_pair(0),
        "pair1": lambda: attend_pair(1),
        "pair2": lambda: attend_pair(2),
        "pair3": lambda: attend_pair(3),
        "out": out_grad,
        "qkv0": lambda: qkv_grad(0),
        "qkv1": lambda: qkv_grad(1),
        "qkv2": lambda: qkv_grad(2),
        "swapqkv": lambda: swap_wait(qkv_swaps),
        "land0": lambda: take_land(0),
        "land1": lambda: take_land(1),
        "totals": totals,
        "last": last,
    }
    for item in plan["schedule"]:
        if item in steps:
            steps[item]()
        elif summed:
            next(flows[item], None)
    if not summed:
        for k, (src, dst) in enumerate(zip((g_back, g_in, g_out, g_qkv), (back_res, in_res, out_res, qkv_res))):
            c = pltpu.make_async_copy(src, dst, own_sems.at[k])
            c.start()
            c.wait()
    for c in late[-2:]:
        c.wait()
    for build in stage_sends.values():
        build().wait_send()
    core.finish()
    wire.finish()


COMPUTE = [
    "feed0", "feed1", "swap01", "feed2", "feed3", "swap23", "close", "project",
    "pair0", "pair1", "pair2", "pair3", "out", "qkv0", "qkv1", "qkv2", "swapqkv",
    "totals", "last",
]


def ticks_of(lengths):
    return 2 * sum(1 if n == 2 else n - 1 for n in lengths) + 1


def make_plan(lines):
    lengths = [n for _, n in lines]
    orders = ORDERS
    ticks = ticks_of(lengths)
    spots, top = [], 0
    spare = {"x": [0, 1024], "wb": [512, 2048], "normed": [0, 1024]}
    for u in range(len(UNITS)):
        need = land_rows(TILE, [lengths[i] for i in line_order(orders[u], lines)])
        zone = next((z for z, (a, b) in spare.items() if (z == "x" or u >= FEED_UNITS) and a + need <= b), None)
        if zone:
            spots.append((zone, spare[zone][0]))
            spare[zone][0] += need
        else:
            spots.append(("land", top))
            top += need
    schedule = list(COMPUTE) + ["land0", "land1"]
    names = list(range(len(UNITS))) + ["vec"]
    for _ in range(ticks):
        schedule += names
    return {"orders": orders, "land": spots, "rows": top, "schedule": schedule}


def layout(lengths, row_count):
    slot = jnp.arange(lengths.shape[0])
    upto = slot[:, None] <= slot[None, :]
    ends = jnp.sum(jnp.where(upto, lengths[:, None], 0), axis=0, dtype=jnp.int32)
    place = jnp.arange(row_count, dtype=jnp.int32)
    passed = (place[:, None] >= ends[None, :]).astype(jnp.int32)
    segment = jnp.sum(passed, axis=1, dtype=jnp.int32)
    starts = jnp.sum(passed * lengths[None, :], axis=1, dtype=jnp.int32)
    live = place < ends[-1]
    code = jnp.where(live, segment, PAD_CODE + place)
    return code, (place - starts).astype(F32)


def tables(position, width):
    column = jnp.arange(width, dtype=jnp.int32) % HEAD_DIM
    pair_index = (column // 2).astype(F32)
    frequency = jnp.exp(pair_index * (-2.0 * math.log(10000.0) / ROT))
    angles = position[:, None] * frequency[None, :]
    rotated = (column < ROT)[None, :]
    sign_flip = jnp.where(column % 2 == 0, -1.0, 1.0)[None, :]
    return (
        jnp.where(rotated, jnp.cos(angles), 1.0),
        jnp.where(rotated, jnp.sin(angles) * sign_flip, 0.0),
    )


def on_device(
    lines_at,
    block_input,
    cotangent,
    seq_lengths,
    layer_norm_gain,
    layer_norm_bias,
    qkv_weight,
    out_weight,
    in_weight,
    in_bias,
    back_weight,
    back_bias,
):
    rows, half = block_input.shape
    full = 2 * half
    code, position = layout(seq_lengths[0], rows)
    cosine, sine = tables(position, PAIR)
    small = jnp.concatenate(
        [
            layer_norm_gain[None],
            layer_norm_bias[None],
            back_bias[None],
            jnp.zeros((13, half), BF16),
        ],
        axis=0,
    )
    lengths = [n for _, n in lines_at]
    total = 1
    for n in lengths:
        total *= n
    summed = TILE % (16 * total) == 0 and len(lengths) <= 3
    plan = make_plan(lines_at)
    n_sems = max(1, 2 * sum(line_sems(n) for n in lengths) * len(UNITS) + sum(line_sems(n) for n in lengths))
    slot_rows = [16 * n for n in lengths] + [16, 16, 16]
    vmem, anyw = pl.BlockSpec(memory_space=pltpu.VMEM), pl.BlockSpec(memory_space=pl.ANY)
    outs = pl.pallas_call(
        functools.partial(kernel, lines_at, summed, plan),
        out_shape=(
            jax.ShapeDtypeStruct((rows, half), BF16),
            jax.ShapeDtypeStruct((rows, half), BF16),
            jax.ShapeDtypeStruct((16, TILE), F32),
            jax.ShapeDtypeStruct((4 * half, full), BF16),
            jax.ShapeDtypeStruct((half, 8 * half), BF16),
            jax.ShapeDtypeStruct((half, full), BF16),
            jax.ShapeDtypeStruct((half, 6 * half), BF16),
            jax.ShapeDtypeStruct((half, 3 * half), BF16),
            jax.ShapeDtypeStruct((rows, half), BF16),
        ),
        in_specs=[anyw] * 6 + [vmem] * 6,
        out_specs=[anyw] * 2 + [vmem] + [anyw] * 6,
        scratch_shapes=[
            pltpu.VMEM((rows, full), BF16),
            pltpu.VMEM((rows, full), BF16),
            pltpu.VMEM((rows, full), BF16),
            pltpu.VMEM((full, rows), BF16),
            pltpu.VMEM((full, 4 * half), BF16),
            pltpu.VMEM((4 * half, full), BF16),
            pltpu.VMEM((rows, 4 * half), BF16),
            pltpu.VMEM((rows, 4 * half), BF16),
            pltpu.VMEM((rows, full), BF16),
            pltpu.VMEM((rows, full), BF16),
            pltpu.VMEM((2, half, 512), BF16),
            pltpu.VMEM((TILE, rows), BF16),
            pltpu.VMEM((2, rows, PAIR), F32),
            pltpu.VMEM((2, 16, half), BF16),
            pltpu.VMEM((4 * half, full), BF16),
            pltpu.VMEM((half, 8 * half), BF16),
            pltpu.VMEM((half, full), BF16),
            pltpu.VMEM((half, 6 * half), BF16),
            pltpu.VMEM((plan["rows"] if summed else 16, 1024), BF16),
            pltpu.VMEM((slot_rows[0], TILE), F32),
            pltpu.VMEM((slot_rows[1], TILE), F32),
            pltpu.VMEM((slot_rows[2], TILE), F32),
            pltpu.SemaphoreType.DMA((24,)),
            pltpu.SemaphoreType.DMA((24,)),
            pltpu.SemaphoreType.DMA((16,)),
            pltpu.SemaphoreType.DMA((n_sems,)),
            pltpu.SemaphoreType.DMA((n_sems,)),
            pltpu.SemaphoreType.DMA((len(UNITS),)),
            pltpu.SemaphoreType.REGULAR,
            pltpu.SemaphoreType.REGULAR((2,)),
        ],
        compiler_params=pltpu.CompilerParams(
            collective_id=0, has_side_effects=True, vmem_limit_bytes=60 * 2**20
        ),
    )(
        block_input,
        cotangent,
        qkv_weight,
        out_weight,
        in_weight,
        back_weight,
        small,
        in_bias.astype(F32).reshape(8, TILE),
        code[:, None],
        code[None, :],
        cosine,
        sine,
    )
    block_output, input_grad, vec, back_grad, in_grad, out_grad, qkv_grad, _, _ = outs
    if not summed:
        vec, back_grad, in_grad, out_grad, qkv_grad = (
            lax.psum(v, "dp") for v in (vec, back_grad, in_grad, out_grad, qkv_grad)
        )
    return (
        block_output,
        input_grad,
        vec[10:12].reshape(half),
        vec[12:14].reshape(half),
        qkv_grad.astype(F32),
        out_grad.astype(F32),
        in_grad.astype(F32),
        vec[0:8].reshape(4 * half),
        back_grad.astype(F32),
        vec[8:10].reshape(half),
    )


def solution(mesh):
    wide, vector = P("branch", None), P("branch")
    tokens = P("dp", "branch")
    return jax.shard_map(
        functools.partial(on_device, dp_lines(mesh)),
        mesh=mesh,
        in_specs=(
            tokens, tokens, P("dp", None), vector, vector, wide, wide, wide, vector, wide, vector,
        ),
        out_specs=(tokens, tokens, vector, vector, wide, wide, wide, vector, wide, vector),
        check_vma=False,
    )
```

```python
import functools
import math

import jax
import jax.numpy as jnp
from jax import lax
from jax.experimental import pallas as pl
from jax.experimental.pallas import tpu as pltpu
from jax.sharding import PartitionSpec as P

HEAD_DIM = 64
ROT = 32
NORM_EPSILON = 1e-05
MASKED = -1e30
PAD_CODE = 1 << 16
TILE = 256
PAIR = 128
MESH = pl.DeviceIdType.MESH
F32 = jnp.float32
BF16 = jnp.bfloat16
ROOT = math.sqrt(2.0 / math.pi)
CUBIC = 0.044715


def ds(start, size):
    if not isinstance(start, int):
        for unit in (1024, 512, 256, 128, 64, 32, 16, 8):
            if size % unit == 0:
                start = pl.multiple_of(start, unit)
                break
    return pl.ds(start, size)


def dot(a, b):
    return lax.dot_general(a, b, (((1,), (0,)), ((), ())), preferred_element_type=F32)


def dot_nt(a, b):
    return lax.dot_general(a, b, (((1,), (1,)), ((), ())), preferred_element_type=F32)


def dot_tn(a, b):
    return lax.dot_general(a, b, (((0,), (0,)), ((), ())), preferred_element_type=F32)


def loop(count, body):
    def step(i, carry):
        body(i)
        return carry

    lax.fori_loop(0, count, step, 0)


def inside(value, count):
    return (value >= 0) & (value < count)


def dp_lines(mesh):
    count = mesh.shape["dp"]
    places = [getattr(d, "coords", None) for d in mesh.devices[0]]
    lines = []
    if all(p is not None for p in places):
        for axis in range(3):
            length = len({p[axis] for p in places})
            if length > 1:
                first = next(i for i in range(count) if places[i][axis] != places[0][axis])
                lines.append((first, length))
        lines.sort()
        stride = 1
        for s, n in lines:
            if s != stride:
                lines = []
                break
            stride *= n
        if lines and stride == count:
            return lines
    lines, stride = [], 1
    while stride < count:
        lines.append((stride, 2))
        stride *= 2
    return lines


class Line:
    def __init__(self, dp, stride, length):
        self.dp, self.stride, self.length = dp, stride, length
        self.place = lax.rem(lax.div(dp, stride), length)

    def at(self, step):
        return {"dp": self.dp + step * self.stride}


def line_sems(length):
    return 1 if length == 2 else 2 * (length - 1)


def land_rows(rows, lengths):
    need = 0
    for length in lengths:
        rows //= length
        need += rows * line_sems(length)
    return need


class Wire:
    def __init__(self, send, recv):
        self.send, self.recv, self.used, self.sent = send, recv, 0, []

    def take(self):
        self.used += 1
        return self.used - 1

    def copy(self, src, dst, sem, to):
        return pltpu.make_async_remote_copy(
            src_ref=src,
            dst_ref=dst,
            send_sem=self.send.at[sem],
            recv_sem=self.recv.at[sem],
            device_id=to,
            device_id_type=MESH,
        )

    def finish(self):
        for can, build in self.sent:
            if can is None:
                build().wait_send()
            else:
                pl.when(can)(lambda build=build: build().wait_send())
        self.sent = []


class Rows:
    def __init__(self, ref, column, width):
        self.ref, self.column, self.width = ref, column, width

    def at(self, row, rows):
        return self.ref.at[ds(row, rows), pl.ds(self.column, self.width)]

    def load(self, row, rows):
        return self.ref[ds(row, rows), pl.ds(self.column, self.width)]

    def store(self, row, rows, value):
        self.ref[ds(row, rows), pl.ds(self.column, self.width)] = value


def add_rows(block, base, land, off, rows):
    step = next(s for s in (64, 48, 32, 16) if rows % s == 0)

    even = math.gcd(off, step)

    def body(i):
        mine = block.load(base + i * step, step).astype(F32)
        at = pl.multiple_of(off + i * step, even) if even > 1 and not isinstance(i, int) else off
        other = land.ref[pl.ds(at, step), pl.ds(land.column, land.width)].astype(F32)
        block.store(base + i * step, step, (mine + other).astype(BF16))

    if rows == step:
        body(0)
    else:
        loop(rows // step, body)


def sum_line(wire, line, block, base, rows, land, off):
    length, p = line.length, line.place
    blk = rows // length
    if length == 2:
        sem = wire.take()
        other = 1 - p

        def build():
            return wire.copy(
                block.at(base + other * blk, blk), land.at(off, blk), sem, line.at(1 - 2 * p)
            )

        build().start()
        wire.sent.append((None, build))
        yield
        build().wait_recv()
        add_rows(block, base + p * blk, land, off, blk)
        return
    for s in range(1, length):
        r = length - s
        todo = []
        for d in (-1, 1):
            sem = wire.take()
            low = off + (2 * (s - 1) + (d > 0)) * blk

            def build(owner, d=d, sem=sem, low=low):
                return wire.copy(
                    block.at(base + owner * blk, blk), land.at(low, blk), sem, line.at(d)
                )

            can = inside(p + d * r, length)
            goes = functools.partial(build, p + d * r)
            pl.when(can)(lambda goes=goes: goes().start())
            wire.sent.append((can, goes))
            todo.append((d, build, low))
        yield
        for d, build, low in todo:
            owner = p - d + d * r

            def arrive(build=build, owner=owner, low=low):
                build(owner).wait_recv()
                add_rows(block, base + owner * blk, land, low, blk)

            pl.when(inside(p - d, length) & inside(owner, length))(arrive)


def spread_line(wire, line, out, base, blk, first=None):
    length, p = line.length, line.place
    if length == 2:
        sem = wire.take()

        def build(owner, source=None):
            there = out.at(base + owner * blk, blk)
            return wire.copy(there if source is None else source, there, sem, line.at(1 - 2 * p))

        goes = functools.partial(build, p, first)
        goes().start()
        wire.sent.append((None, goes))
        yield
        build(1 - p).wait_recv()
        return
    for r in range(1, length):
        todo = []
        for d in (-1, 1):
            sem = wire.take()

            def build(owner, source=None, d=d, sem=sem):
                there = out.at(base + owner * blk, blk)
                return wire.copy(there if source is None else source, there, sem, line.at(d))

            owner = p - d * (r - 1)
            can = inside(owner, length) & inside(p + d, length)
            goes = functools.partial(build, owner, first if r == 1 else None)
            pl.when(can)(lambda goes=goes: goes().start())
            wire.sent.append((can, goes))
            todo.append((d, build))
        yield
        for d, build in todo:
            owner = p - d * r
            pl.when(inside(owner, length))(
                lambda build=build, owner=owner: build(owner).wait_recv()
            )


def unit_flow(wire, order, block, row, rows, land, off, out, local_sem):
    base, size, spots = row, rows, []
    for line in order:
        yield from sum_line(wire, line, block, base, size, land, off)
        size //= line.length
        off += size * line_sems(line.length)
        spots.append((base, size))
        base = base + line.place * size
    own = pltpu.make_async_copy(block.at(base, size), out.at(base, size), local_sem)
    own.start()
    first = block.at(base, size)
    for line, (start, blk) in list(zip(order, spots))[::-1]:
        yield from spread_line(wire, line, out, start, blk, first)
        if first is not None:
            own.wait()
        first = None


def vector_flow(wire, lines, vec, slots):
    for line, slot in zip(lines, slots):
        rows = vec.shape[0]
        slot[ds(line.place * rows, rows), :] = vec[...]
        yield from spread_line(wire, line, Rows(slot, 0, slot.shape[1]), 0, rows)
        total = slot[0:rows, :]
        for k in range(1, line.length):
            total = total + slot[k * rows : (k + 1) * rows, :]
        vec[...] = total


BACK, IN, OUT, QKV = 0, 1, 2, 3


def make_units():
    units = []
    for block in range(8):
        units.append((BACK, TILE * block, 0))
        if block % 4 == 3:
            for c in (block // 4, 2 + block // 4):
                units += [(IN, 0, 1024 * c), (IN, 256, 1024 * c)]
    units += [(OUT, 0, 0), (OUT, 256, 0)]
    for c in range(3):
        units += [(QKV, 0, 1024 * c), (QKV, 256, 1024 * c)]
    return units


UNITS = make_units()
FEED_UNITS = 16
ORDERS = "XYZXYZXYZXYZXYWXXYXVZXVZ"


def line_order(letter, lines):
    named = {"X": (0, 1, 2), "Y": (1, 0, 2), "Z": (2, 0, 1), "W": (2, 1, 0), "U": (0, 2, 1), "V": (1, 2, 0)}
    return [i for i in named[letter] if i < len(lines)]


def rotate_pairs(values, even):
    return jnp.where(
        even, pltpu.roll(values, PAIR - 1, axis=1), pltpu.roll(values, 1, axis=1)
    )


def kernel(
    lines_at,
    summed,
    plan,
    x_hbm,
    cot_hbm,
    qkv_hbm,
    out_hbm,
    in_hbm,
    back_hbm,
    small_ref,
    in_bias_ref,
    code_col,
    code_row,
    cosine,
    sine,
    block_out,
    input_grad,
    vec,
    back_res,
    in_res,
    out_res,
    qkv_res,
    qkv_other,
    x_far,
    x,
    cot,
    normed,
    turned,
    wa,
    wb,
    act,
    gh,
    mix,
    gn,
    stage,
    act_t,
    acc,
    small,
    g_back,
    g_in,
    g_out,
    g_qkv,
    land,
    slots_x,
    slots_y,
    slots_z,
    core_send,
    core_recv,
    local,
    send,
    recv,
    own_sems,
    core_free,
    land_free,
):
    rows = x.shape[0]
    half = x.shape[1] // 2
    side = lax.axis_index("branch")
    dp = lax.axis_index("dp")
    mate = {"branch": 1 - side}
    lines = [Line(dp, s, n) for s, n in lines_at]
    core = Wire(core_send, core_recv)
    wire = Wire(send, recv)
    mine, theirs = side * half, (1 - side) * half

    barrier = pltpu.get_barrier_semaphore()
    pl.semaphore_signal(barrier, inc=1, device_id=mate, device_id_type=MESH)
    greeted = jnp.int32(1)

    def each_neighbour(visit):
        count = jnp.int32(0)
        for line in lines:
            for d in (-1, 1):
                there = inside(line.place + d, line.length)
                pl.when(there)(lambda line=line, d=d: visit(line.at(d)))
                count = count + there.astype(jnp.int32)
        return count

    if summed:
        greeted = greeted + each_neighbour(
            lambda to: pl.semaphore_signal(barrier, inc=1, device_id=to, device_id_type=MESH)
        )

    loads = []

    def load(src, dst):
        c = pltpu.make_async_copy(src, dst, local.at[len(loads)])
        c.start()
        loads.append(c)
        return c

    x_in = load(x_hbm, x.at[:, ds(mine, half)])
    in_in = load(in_hbm.at[:, ds(side * 4 * half, 4 * half)], wa.at[ds(mine, half), :])
    cot_in = load(cot_hbm, cot.at[:, ds(mine, half)])
    back_in = load(back_hbm, wb)
    pl.semaphore_wait(barrier, greeted)

    def to_mate(src, dst):
        sem = core.take()

        def build():
            return core.copy(src, dst, sem, mate)

        build().start()
        core.sent.append((None, build))
        return build

    def from_mate(build, dst):
        return lambda: build().wait_recv()

    x_other = to_mate(x_hbm, x.at[:, ds(mine, half)])
    small_other = to_mate(small_ref, small.at[1])
    in_other = [
        to_mate(
            in_hbm.at[:, ds((1 - side) * 4 * half + k * 512, 512)],
            wa.at[ds(mine, half), pl.ds(k * 512, 512)],
        )
        for k in range(4)
    ]
    cot_other = to_mate(cot_hbm, cot.at[:, ds(mine, half)])
    qkv_far = [
        to_mate(
            qkv_hbm.at[:, ds(k * 2 * half + theirs, half)],
            qkv_other.at[:, pl.ds(k * half, half)],
        )
        for k in range(3)
    ]

    x_again = to_mate(x_hbm, x_far)

    x_in.wait()
    x_other().wait_recv()
    small_other().wait_recv()
    gain_mine = small_ref[0:1, :].astype(F32)
    shift_mine = small_ref[1:2, :].astype(F32)
    gain_other = small[1, 0:1, :].astype(F32)
    shift_other = small[1, 1:2, :].astype(F32)
    first = side == 0

    def both(own, other):
        return jnp.concatenate(
            [jnp.where(first, own, other), jnp.where(first, other, own)], axis=1
        )

    gain = both(gain_mine, gain_other)
    shift = both(shift_mine, shift_other)

    def standard(values):
        mean = jnp.mean(values, axis=1, keepdims=True)
        centred = values - mean
        variance = jnp.mean(centred * centred, axis=1, keepdims=True)
        scale = lax.rsqrt(variance + NORM_EPSILON)
        return mean, scale, centred * scale

    def norm_tile(i):
        at = ds(i * 128, 128)
        _, _, xhat = standard(x[at, :].astype(F32))
        value = xhat * gain + shift
        normed[at, :] = value.astype(BF16)
        turned[:, at] = value.T.astype(BF16)

    loop(rows // 128, norm_tile)

    def give_land(which):
        if summed:
            each_neighbour(
                lambda to: pl.semaphore_signal(
                    land_free.at[which], inc=1, device_id=to, device_id_type=MESH
                )
            )

    def take_land(which):
        if summed:
            pl.semaphore_wait(land_free.at[which], each_neighbour(lambda to: None))

    give_land(0)
    cot_in.wait()
    cot_other().wait_recv()

    def live_tile(i):
        at = ds(i * 128, 128)
        live = code_col[at, :] < PAD_CODE
        cot[at, :] = jnp.where(live, cot[at, :].astype(F32), 0.0).astype(BF16)

    loop(rows // 128, live_tile)
    in_in.wait()
    back_in.wait()

    stage_sends = {}

    def send_stage(name, slot, view, dst):
        sem = core.take()

        def build():
            return core.copy(view, dst, sem, mate)

        build().start()
        stage_sends[slot] = build
        return build

    def hidden_block(j):
        at = pl.ds(j * TILE, TILE)

        def row_tile(m, total):
            r = ds(m * TILE, TILE)
            hidden = dot(normed[r, :], wa[:, at]) + in_bias_ref[j : j + 1, :]
            square = hidden * hidden
            t = jnp.tanh(ROOT * hidden * (1.0 + CUBIC * square))
            up = 0.5 * (1.0 + t)
            active = hidden * up
            slope = up + 0.5 * hidden * (1.0 - t * t) * (ROOT * (1.0 + 3.0 * CUBIC * square))
            act[r, at] = active.astype(BF16)
            act_t[:, r] = active.T.astype(BF16)
            grad = dot_nt(cot[r, :], wb[at, :]) * slope
            low = grad.astype(BF16)
            gh[r, at] = low
            return total + jnp.sum(low.astype(F32), axis=0, keepdims=True)

        total = lax.fori_loop(0, rows // TILE, row_tile, jnp.zeros((1, TILE), F32))
        vec[j : j + 1, :] = total

        def back_tile(n):
            c = ds(n * TILE, TILE)
            g_back[at, c] = dot(act_t[...], cot[:, c]).astype(BF16)

        loop(2 * half // TILE, back_tile)
        slot = j % 2
        if slot in stage_sends:
            stage_sends[slot]().wait_send()

        def in_tile(n):
            g_in[ds(n * TILE, TILE), ds(side * 4 * half + j * TILE, TILE)] = dot(
                turned[ds(mine + n * TILE, TILE), :], gh[:, at]
            ).astype(BF16)
            stage[slot, ds(n * TILE, TILE), pl.ds(0, TILE)] = dot(
                turned[ds(theirs + n * TILE, TILE), :], gh[:, at]
            ).astype(BF16)

        loop(half // TILE, in_tile)
        return send_stage(
            "in",
            slot,
            stage.at[slot, :, pl.ds(0, TILE)],
            g_in.at[:, ds(side * 4 * half + j * TILE, TILE)],
        )

    in_swaps = []

    def feed(j):
        if j % 2 == 0:
            in_other[j // 2]().wait_recv()
        in_swaps.append(hidden_block(j))

    def swap_wait(builds):
        for build in builds:
            build().wait_recv()

    def feed_out(m):
        r = ds(m * TILE, TILE)
        for n in range(2):
            c = pl.ds(n * 512, 512)
            mix[r, c] = dot(act[r, :], wb[:, c]).astype(BF16)
            gn[r, c] = dot_nt(gh[r, :], wa[c, :]).astype(BF16)

    late = []

    def feed_close():
        loop(rows // TILE, feed_out)
        for build in qkv_far:
            build().wait_recv()
        base = len(loads)
        for k in range(3):
            late.append(
                load(
                    qkv_hbm.at[:, ds(k * 2 * half + mine, half)],
                    wa.at[ds(mine, half), pl.ds(k * half, half)],
                )
            )
        late.append(load(qkv_other, wa.at[ds(theirs, half), pl.ds(0, 3 * half)]))
        late.append(load(out_hbm, wb.at[pl.ds(0, half), :]))
        pl.semaphore_signal(core_free, inc=1, device_id=mate, device_id_type=MESH)

    even = lax.rem(lax.broadcasted_iota(jnp.int32, (1, PAIR), 1), 2) == 0

    def project(m):
        r = ds(m * TILE, TILE)
        cos_t, sin_t = cosine[r, :], sine[r, :]
        for k in range(3):
            made = dot(normed[r, :], wa[:, pl.ds(k * half, half)])
            if k == 2:
                act[r, pl.ds(2 * half, half)] = made.astype(BF16)
                continue
            for c in range(half // PAIR):
                piece = made[:, c * PAIR : (c + 1) * PAIR]
                piece = piece * cos_t + rotate_pairs(piece, even) * sin_t
                if k == 0:
                    piece = piece * HEAD_DIM**-0.5
                act[r, pl.ds(k * half + c * PAIR, PAIR)] = piece.astype(BF16)
        act[r, pl.ds(3 * half, half)] = dot_nt(cot[r, :], wb[pl.ds(0, half), :]).astype(BF16)

    def project_all():
        for c in late:
            c.wait()
        loop(rows // TILE, project)
        give_land(1)

    lane = lax.broadcasted_iota(jnp.int32, (1, PAIR), 1)

    def unrotate(grad, r):
        return grad * cosine[r, :] + rotate_pairs(grad * sine[r, :], even)

    def attend_block(pair, i):
        low = max(0, i - 2) * TILE
        count = (i + 1) * TILE - low
        qr, kr = pl.ds(i * TILE, TILE), pl.ds(low, count)
        qc = ds(pair * PAIR, PAIR)
        kc = ds(half + pair * PAIR, PAIR)
        vc = ds(2 * half + pair * PAIR, PAIR)
        gc = ds(3 * half + pair * PAIR, PAIR)
        q, k, v, g = act[qr, qc], act[kr, kc], act[kr, vc], act[qr, gc]
        same = code_col[qr, :] == code_row[:, kr]
        place_q = i * TILE + lax.broadcasted_iota(jnp.int32, (TILE, count), 0)
        place_k = low + lax.broadcasted_iota(jnp.int32, (TILE, count), 1)
        allowed = same & (place_k <= place_q)
        context = jnp.zeros((TILE, PAIR), F32)
        grad_q = jnp.zeros((TILE, PAIR), F32)
        grad_k = jnp.zeros((count, PAIR), F32)
        grad_v = jnp.zeros((count, PAIR), F32)
        zero = jnp.zeros((), BF16)
        for head in range(2):
            here = (lane >= head * HEAD_DIM) & (lane < (head + 1) * HEAD_DIM)
            kh, vh = jnp.where(here, k, zero), jnp.where(here, v, zero)
            qh, gr = jnp.where(here, q, zero), jnp.where(here, g, zero)
            scores = jnp.where(allowed, dot_nt(q, kh), MASKED)
            top = jnp.max(scores, axis=1, keepdims=True)
            weight = jnp.exp(scores - top)
            weight = weight * (1.0 / jnp.sum(weight, axis=1, keepdims=True))
            weight_low = weight.astype(BF16)
            context = context + dot(weight_low, vh)
            grad_weight = dot_nt(g, vh)
            inner = jnp.sum(weight * grad_weight, axis=1, keepdims=True)
            grad_scores = (weight * (grad_weight - inner)).astype(BF16)
            grad_v = grad_v + dot_tn(weight_low, gr)
            grad_q = grad_q + dot(grad_scores, kh)
            grad_k = grad_k + dot_tn(grad_scores, qh)
        act[qr, gc] = context.astype(BF16)
        act[qr, qc] = unrotate(grad_q * HEAD_DIM**-0.5, qr).astype(BF16)
        fresh = count if i < 1 else TILE
        old = count - TILE
        if old:
            acc[0, pl.ds(low, old), :] += grad_k[:old]
            acc[1, pl.ds(low, old), :] += grad_v[:old]
        acc[0, pl.ds(low + old, TILE), :] = grad_k[old:]
        acc[1, pl.ds(low + old, TILE), :] = grad_v[old:]

    def attend_pair(pair):
        for i in range(rows // TILE):
            attend_block(pair, i)

        def close(m):
            r = ds(m * TILE, TILE)
            act[r, ds(half + pair * PAIR, PAIR)] = unrotate(acc[0, r, :], r).astype(BF16)
            act[r, ds(2 * half + pair * PAIR, PAIR)] = acc[1, r, :].astype(BF16)

        loop(rows // TILE, close)

    def out_grad():
        def tile(n):
            c = ds(n * TILE, TILE)
            g_out[:, c] = dot_tn(act[:, pl.ds(3 * half, half)], cot[:, c]).astype(BF16)

        loop(2 * half // TILE, tile)

    qkv_swaps = []

    def qkv_grad(k):
        slot = k % 2
        if slot in stage_sends:
            stage_sends[slot]().wait_send()

        def tile(n):
            r = ds(n * TILE, TILE)
            right = act[:, pl.ds(k * half, half)]
            g_qkv[r, ds(k * 2 * half + mine, half)] = dot(
                turned[ds(mine + n * TILE, TILE), :], right
            ).astype(BF16)
            stage[slot, r, :] = dot(turned[ds(theirs + n * TILE, TILE), :], right).astype(BF16)

        loop(half // TILE, tile)
        qkv_swaps.append(
            send_stage("qkv", slot, stage.at[slot], g_qkv.at[:, ds(k * 2 * half + mine, half)])
        )

    swaps = []

    def totals():
        x_again().wait_recv()
        late.append(load(x_hbm, turned.at[:, ds(mine, half)]))
        late.append(load(x_far, turned.at[:, ds(theirs, half)]))

        def tile(m):
            r = ds(m * TILE, TILE)
            for n in range(2):
                c = pl.ds(n * 512, 512)
                mix[r, c] = (
                    mix[r, c].astype(F32)
                    + dot(act[r, pl.ds(3 * half, half)], wb[pl.ds(0, half), c])
                ).astype(BF16)
                gn[r, c] = (
                    gn[r, c].astype(F32)
                    + dot_nt(act[r, pl.ds(0, 3 * half)], wa[c, pl.ds(0, 3 * half)])
                ).astype(BF16)

        loop(rows // TILE, tile)
        pl.semaphore_wait(core_free, 1)
        for src, dst in (
            (gn, gh.at[:, pl.ds(0, 2 * half)]),
            (mix.at[:, ds(theirs, half)], gh.at[:, pl.ds(2 * half, half)]),
        ):
            swaps.append(to_mate(src, dst))

    def last():
        for build in swaps:
            build().wait_recv()
        for c in late[-2:]:
            c.wait()
        back_bias = small_ref[2:3, :].astype(F32)
        own = ds(mine, half)

        def tile(m, carry):
            gain_sum, shift_sum, bias_sum = carry
            r = ds(m * 128, 128)
            mean, scale, xhat = standard(turned[r, :].astype(F32))
            x_own = turned[r, own].astype(F32)
            gh[r, pl.ds(3 * half, half)] = (
                x_own
                + (mix[r, own].astype(F32) + gh[r, pl.ds(2 * half, half)].astype(F32) + back_bias)
            ).astype(BF16)
            scaled = (gn[r, :].astype(F32) + gh[r, pl.ds(0, 2 * half)].astype(F32)) * gain
            mean_one = jnp.mean(scaled, axis=1, keepdims=True)
            mean_two = jnp.mean(scaled * xhat, axis=1, keepdims=True)
            grad_own = gn[r, own].astype(F32) + gh[r, own].astype(F32)
            xhat_own = (x_own - mean) * scale
            cot_own = cot[r, own].astype(F32)
            cot[r, own] = (
                cot_own + scale * (grad_own * gain_mine - mean_one - xhat_own * mean_two)
            ).astype(BF16)
            return (
                gain_sum + jnp.sum(grad_own * xhat_own, axis=0, keepdims=True),
                shift_sum + jnp.sum(grad_own, axis=0, keepdims=True),
                bias_sum + jnp.sum(cot_own, axis=0, keepdims=True),
            )

        zero = jnp.zeros((1, half), F32)
        gain_sum, shift_sum, bias_sum = lax.fori_loop(0, rows // 128, tile, (zero, zero, zero))
        for k, value in enumerate((bias_sum, gain_sum, shift_sum)):
            vec[8 + 2 * k : 9 + 2 * k, :] = value[:, :TILE]
            vec[9 + 2 * k : 10 + 2 * k, :] = value[:, TILE:]
        vec[14:16, :] = jnp.zeros((2, TILE), F32)
        late.append(load(gh.at[:, pl.ds(3 * half, half)], block_out))
        late.append(load(cot.at[:, ds(mine, half)], input_grad))

    results = {BACK: back_res, IN: in_res, OUT: out_res, QKV: qkv_res}
    grads = {BACK: g_back, IN: g_in, OUT: g_out, QKV: g_qkv}
    flows = {}
    if summed:
        off = 0
        lengths = [n for _, n in lines_at]
        for u, (kind, row, column) in enumerate(UNITS):
            order = line_order(plan["orders"][u], lines_at)
            need = land_rows(TILE, [lengths[i] for i in order])
            where = plan["land"][u]
            zone = Rows({"land": land, "wb": wb, "normed": normed, "x": x}[where[0]], 0, 1024)
            flows[u] = unit_flow(
                wire,
                [lines[i] for i in order],
                Rows(grads[kind], column, 1024),
                row,
                TILE,
                zone,
                where[1],
                Rows(results[kind], column, 1024),
                own_sems.at[u],
            )
        flows["vec"] = vector_flow(wire, lines, vec, (slots_x, slots_y, slots_z)[: len(lines)])

    steps = {
        "swap0": lambda: swap_wait(in_swaps[0:4]),
        "swap1": lambda: swap_wait(in_swaps[4:8]),
        "close": feed_close,
        "project": project_all,
        "pair0": lambda: attend_pair(0),
        "pair1": lambda: attend_pair(1),
        "pair2": lambda: attend_pair(2),
        "pair3": lambda: attend_pair(3),
        "out": out_grad,
        "qkv0": lambda: qkv_grad(0),
        "qkv1": lambda: qkv_grad(1),
        "qkv2": lambda: qkv_grad(2),
        "swapq": lambda: swap_wait(qkv_swaps[0:1]),
        "swapk": lambda: swap_wait(qkv_swaps[1:2]),
        "swapv": lambda: swap_wait(qkv_swaps[2:3]),
        "land0": lambda: take_land(0),
        "land1": lambda: take_land(1),
        "totals": totals,
        "last": last,
    }
    for j in range(8):
        steps[f"hid{j}"] = functools.partial(feed, j)
    for item in plan["schedule"]:
        if item in steps:
            steps[item]()
        elif summed:
            next(flows[item], None)
    while flows:
        for name in list(flows):
            if next(flows[name], "end") == "end":
                del flows[name]
    if not summed:
        for k, (src, dst) in enumerate(zip((g_back, g_in, g_out, g_qkv), (back_res, in_res, out_res, qkv_res))):
            c = pltpu.make_async_copy(src, dst, own_sems.at[k])
            c.start()
            c.wait()
    for c in late[-2:]:
        c.wait()
    for build in stage_sends.values():
        build().wait_send()
    core.finish()
    wire.finish()


COMPUTE = [
    "hid0", "hid1", "hid2", "hid3", "swap0", "hid4", "hid5", "hid6", "hid7", "swap1",
    "close", "project", "pair0", "pair1", "pair2", "pair3",
    "out", "qkv0", "qkv1", "qkv2", "swapq", "swapk", "swapv", "totals", "last",
]
ORDER = (
    -1, 0, -2, 1, -3, 0, 2, -4, 1, 2, 3, 0, 4, 5, 6, 7, -6, 0, 1, 2, 8, -7, 0, 1, 3, 4, 5, 9, -8, 0, 1, 2, 3, 6,
    7, 8, 10, -9, 0, 1, 3, 4, 5, 6, 11, 12, 9, 8, 13, 14, 15, 0, -11, 0, 1, 2, 3, 4, 5, 6, 7, 9, 8, 10, 11, 12, 1,
    13, -12, 0, 1, 2, 3, 4, 5, 6, 8, 7, 9, 12, 14, 15, -13, 2, 3, 4, 5, 6, 8, 7, 9, 12, 10, 11, 13, 14, 0, 3, 15,
    5, -14, 1, 2, 5, 4, 6, 8, 7, 9, 12, 10, 11, 3, 13, -15, 1, 2, 5, 4, 6, 8, 7, 11, 3, 14, 9, 15, -16, 3, 2, 4,
    5, 6, 11, 12, 10, 13, 14, -17, 8, 16, 17, 7, -18, 4, 6, 9, 11, 14, 15, 18, 19, -19, 2, 20, 21, -20, 5, 22, 12,
    16, 17, 10, 23, -24, 8, 6, 7, 4, 9, 13, 15, 20, 23, 11, 12, -25, 8, 10, 13, 14, 19, 15, 20, 18, 23, 12, 22,
    11, 10, 21, 13, 19, 15, 16, 17, 20, 9, 14, 7, 23, 20, 22, 10, 18, 13, 15, 11, 16, 17, 19, 12, 9, 14, 21, 23,
    11, 18, 22, 16, 17, 10, 19, 21, 7, 13, 20, 14, 18, 22, 15, 16, 23, 17, 21, 14, 12, 18, 19, 16, 22, 17, 21, 18,
    10, 16, 17, 21, 18, 16, 15, 17, 19, 21, 22, 18, 13, 20, 19, 23, 21, 17, 22, 20, 16, 19, 23, 22, 18, 20, 21,
    19, 16, 23, 22, 17, 18, 20, 23, 19, 21, 20, 23, 22,
)


def make_plan(lines):
    lengths = [n for _, n in lines]
    spots, top = [], 0
    spare = {"x": [0, 1024], "wb": [512, 2048], "normed": [0, 1024]}
    for u in range(len(UNITS)):
        need = land_rows(TILE, [lengths[i] for i in line_order(ORDERS[u], lines)])
        zone = next((z for z, (a, b) in spare.items() if (z == "x" or u >= FEED_UNITS) and a + need <= b), None)
        if zone:
            spots.append((zone, spare[zone][0]))
            spare[zone][0] += need
        else:
            spots.append(("land", top))
            top += need
    schedule, seen = [], set()

    def once(name):
        if name not in seen:
            seen.add(name)
            schedule.append(name)

    for item in ORDER:
        if item < 0:
            once(COMPUTE[-1 - item])
            continue
        once("land0" if item < FEED_UNITS else "land1")
        kind, _, column = UNITS[item]
        if kind == IN:
            once("swap0" if item < FEED_UNITS // 2 else "swap1")
        if kind == QKV:
            once("swap" + "qkv"[column // 1024])
        schedule.append(item)
    for name in COMPUTE + ["land0", "land1"]:
        once(name)
    return {"orders": ORDERS, "land": spots, "rows": top, "schedule": schedule + ["vec"] * 12}


def layout(lengths, row_count):
    slot = jnp.arange(lengths.shape[0])
    upto = slot[:, None] <= slot[None, :]
    ends = jnp.sum(jnp.where(upto, lengths[:, None], 0), axis=0, dtype=jnp.int32)
    place = jnp.arange(row_count, dtype=jnp.int32)
    passed = (place[:, None] >= ends[None, :]).astype(jnp.int32)
    segment = jnp.sum(passed, axis=1, dtype=jnp.int32)
    starts = jnp.sum(passed * lengths[None, :], axis=1, dtype=jnp.int32)
    live = place < ends[-1]
    code = jnp.where(live, segment, PAD_CODE + place)
    return code, (place - starts).astype(F32)


def tables(position, width):
    column = jnp.arange(width, dtype=jnp.int32) % HEAD_DIM
    pair_index = (column // 2).astype(F32)
    frequency = jnp.exp(pair_index * (-2.0 * math.log(10000.0) / ROT))
    angles = position[:, None] * frequency[None, :]
    rotated = (column < ROT)[None, :]
    sign_flip = jnp.where(column % 2 == 0, -1.0, 1.0)[None, :]
    return (
        jnp.where(rotated, jnp.cos(angles), 1.0),
        jnp.where(rotated, jnp.sin(angles) * sign_flip, 0.0),
    )


def on_device(
    lines_at,
    block_input,
    cotangent,
    seq_lengths,
    layer_norm_gain,
    layer_norm_bias,
    qkv_weight,
    out_weight,
    in_weight,
    in_bias,
    back_weight,
    back_bias,
):
    rows, half = block_input.shape
    full = 2 * half
    code, position = layout(seq_lengths[0], rows)
    cosine, sine = tables(position, PAIR)
    small = jnp.concatenate(
        [
            layer_norm_gain[None],
            layer_norm_bias[None],
            back_bias[None],
            jnp.zeros((13, half), BF16),
        ],
        axis=0,
    )
    lengths = [n for _, n in lines_at]
    total = 1
    for n in lengths:
        total *= n
    summed = TILE % (16 * total) == 0 and len(lengths) <= 3
    plan = make_plan(lines_at)
    n_sems = max(1, 2 * sum(line_sems(n) for n in lengths) * len(UNITS) + sum(line_sems(n) for n in lengths))
    slot_rows = [16 * n for n in lengths] + [16, 16, 16]
    vmem, anyw = pl.BlockSpec(memory_space=pltpu.VMEM), pl.BlockSpec(memory_space=pl.ANY)
    outs = pl.pallas_call(
        functools.partial(kernel, lines_at, summed, plan),
        out_shape=(
            jax.ShapeDtypeStruct((rows, half), BF16),
            jax.ShapeDtypeStruct((rows, half), BF16),
            jax.ShapeDtypeStruct((16, TILE), F32),
            jax.ShapeDtypeStruct((4 * half, full), BF16),
            jax.ShapeDtypeStruct((half, 8 * half), BF16),
            jax.ShapeDtypeStruct((half, full), BF16),
            jax.ShapeDtypeStruct((half, 6 * half), BF16),
            jax.ShapeDtypeStruct((half, 3 * half), BF16),
            jax.ShapeDtypeStruct((rows, half), BF16),
        ),
        in_specs=[anyw] * 6 + [vmem] * 6,
        out_specs=[anyw] * 2 + [vmem] + [anyw] * 6,
        scratch_shapes=[
            pltpu.VMEM((rows, full), BF16),
            pltpu.VMEM((rows, full), BF16),
            pltpu.VMEM((rows, full), BF16),
            pltpu.VMEM((full, rows), BF16),
            pltpu.VMEM((full, 4 * half), BF16),
            pltpu.VMEM((4 * half, full), BF16),
            pltpu.VMEM((rows, 4 * half), BF16),
            pltpu.VMEM((rows, 4 * half), BF16),
            pltpu.VMEM((rows, full), BF16),
            pltpu.VMEM((rows, full), BF16),
            pltpu.VMEM((2, half, 512), BF16),
            pltpu.VMEM((TILE, rows), BF16),
            pltpu.VMEM((2, rows, PAIR), F32),
            pltpu.VMEM((2, 16, half), BF16),
            pltpu.VMEM((4 * half, full), BF16),
            pltpu.VMEM((half, 8 * half), BF16),
            pltpu.VMEM((half, full), BF16),
            pltpu.VMEM((half, 6 * half), BF16),
            pltpu.VMEM((plan["rows"] if summed else 16, 1024), BF16),
            pltpu.VMEM((slot_rows[0], TILE), F32),
            pltpu.VMEM((slot_rows[1], TILE), F32),
            pltpu.VMEM((slot_rows[2], TILE), F32),
            pltpu.SemaphoreType.DMA((24,)),
            pltpu.SemaphoreType.DMA((24,)),
            pltpu.SemaphoreType.DMA((16,)),
            pltpu.SemaphoreType.DMA((n_sems,)),
            pltpu.SemaphoreType.DMA((n_sems,)),
            pltpu.SemaphoreType.DMA((len(UNITS),)),
            pltpu.SemaphoreType.REGULAR,
            pltpu.SemaphoreType.REGULAR((2,)),
        ],
        compiler_params=pltpu.CompilerParams(
            collective_id=0, has_side_effects=True, vmem_limit_bytes=60 * 2**20
        ),
    )(
        block_input,
        cotangent,
        qkv_weight,
        out_weight,
        in_weight,
        back_weight,
        small,
        in_bias.astype(F32).reshape(8, TILE),
        code[:, None],
        code[None, :],
        cosine,
        sine,
    )
    block_output, input_grad, vec, back_grad, in_grad, out_grad, qkv_grad, _, _ = outs
    if not summed:
        vec, back_grad, in_grad, out_grad, qkv_grad = (
            lax.psum(v, "dp") for v in (vec, back_grad, in_grad, out_grad, qkv_grad)
        )
    return (
        block_output,
        input_grad,
        vec[10:12].reshape(half),
        vec[12:14].reshape(half),
        qkv_grad.astype(F32),
        out_grad.astype(F32),
        in_grad.astype(F32),
        vec[0:8].reshape(4 * half),
        back_grad.astype(F32),
        vec[8:10].reshape(half),
    )


def solution(mesh):
    wide, vector = P("branch", None), P("branch")
    tokens = P("dp", "branch")
    return jax.shard_map(
        functools.partial(on_device, dp_lines(mesh)),
        mesh=mesh,
        in_specs=(
            tokens, tokens, P("dp", None), vector, vector, wide, wide, wide, vector, wide, vector,
        ),
        out_specs=(tokens, tokens, vector, vector, wide, wide, wide, vector, wide, vector),
        check_vma=False,
    )
```
